256 devices in a mesh: rows: 256 (over x, z, y, core).
Axes of the slice: x: 4, y: 4, z: 8, core: 2. Of those that a mesh axis runs over, the one named last changes fastest.
Arguments:
- x_states: bfloat16 [131072, 2048], P('rows'), may hold values from -6 to 6
- h_blocks: bfloat16 [1024, 12, 128, 128], P('rows'), may hold values from -0.15625 to 0.15625
- col_blocks: int32 [1024, 12], P('rows'), may hold values from 0 to 1023, as said below
- send_list: int32 [256, 4, 4], replicated, may hold values from 0 to 4, as said below
- center: float32 [1], replicated, may hold values from 0.2 to 0.6
- half_width: float32 [1], replicated, may hold values from 1 to 1.5
- rotation: bfloat16 [2048, 2048], P('rows'), may hold values from -0.125 to 0.125
Outputs:
- rotated: bfloat16 [131072, 2048], P('rows')
The draws below stay inside these ranges and needn't reach their ends.
Inputs may be any that keep to these rules, and one draw needn't show every extreme that they name: `col_blocks`: row block b names 12 distinct column blocks (b + t) modulo 1024 with -(6) <= t <= 6, among them those with t = 0, 1, -1, 4, -4, 5 and -5. send_list[o, j] lists in ascending order each p for which block o * 4 + p is named by some row block of the device at offset 1, 2, -1, -2 (j = 0, 1, 2, 3) from device o, modulo the number of devices, and 4 in the remaining places; the lists for offsets 1 and -1 are always full, those for offsets 2 and -2 hold at most 2 blocks, and some device's hold 2.
All inputs are finite; a program needn't handle non-finite values.
Results may differ from the reference program's by a relative error of at most 0.0056.
Values may be sent and summed in bfloat16 or wider, within the bound.
No kernel may reach another device: no remote copies, remote signals or barrier semaphores. Data moves between devices by JAX's collectives and lax.ppermute only.
A program may use at most 128 MiB of HBM per device.

```python
import jax
import jax.numpy as jnp
from jax import lax

BLK = 128
S = 2048
NNZ = 12
B_DEV = 4
NB = 1024
ORDER = 131072


def pattern(key):
    reach = B_DEV + 2
    axis_count = NB // B_DEV
    offsets = jnp.arange(-reach, reach + 1, dtype=jnp.int32)
    row_index = jnp.arange(NB, dtype=jnp.int32)[:, None]
    common = (offsets == 0) | (jnp.abs(offsets) == 1) | (jnp.abs(offsets) == B_DEV) | (jnp.abs(offsets) == B_DEV + 1)
    upper = (row_index == B_DEV - 1) & (offsets[None, :] == reach)
    lower = (row_index == 0) & (offsets[None, :] == -reach)
    forced = common[None, :] | upper | lower
    noise = jax.random.randint(key, (NB, 2 * reach + 1), 0, 1 << 20, dtype=jnp.int32)
    scores = noise * 128 + (offsets + reach)[None, :] + forced.astype(jnp.int32) * (1 << 28)
    top_scores, chosen = lax.top_k(scores, NNZ)
    columns = jnp.mod(row_index + offsets[chosen], NB).astype(jnp.int32)
    owner_device = columns // B_DEV
    local_index = columns - owner_device * B_DEV
    offset = jnp.mod(row_index // B_DEV - owner_device + 2, axis_count) - 2
    list_slot = jnp.where(offset > 0, offset - 1, 1 - offset)
    list_slot = jnp.where(offset == 0, 4, list_slot).astype(jnp.int32)
    needed = jnp.zeros((axis_count, 5, B_DEV), jnp.int32).at[owner_device, list_slot, local_index].max(1)
    needed = needed[:, :4]
    ranked = jnp.where(needed > 0, jnp.arange(B_DEV, dtype=jnp.int32)[None, None, :], B_DEV)
    return (columns, jnp.sort(ranked, axis=-1).astype(jnp.int32))


def draw_col_blocks(key, part):
    return pattern(key)[0]


def draw_send_list(key, part):
    return pattern(key)[1]


def block_scale(own_key, dims, split, least, high):
    def one(position, parts):
        steps = jax.random.uniform(jax.random.fold_in(jax.random.fold_in(own_key, 6), position), (parts,), jnp.float32, least / len(split), high / len(split))
        return jnp.repeat(jnp.exp(steps), dims[position] // parts).reshape((-1,) + (1,) * (len(dims) - position - 1))

    gain = one(*split[0])
    for cut in split[1:]:
        gain = gain * one(*cut)
    return gain


def bell_draw(stream_key, dims, width, limit, cuts=(), kind=jnp.bfloat16):
    drawn = width * jax.random.normal(stream_key, dims, jnp.float32)
    if cuts:
        drawn = drawn * block_scale(stream_key, dims, cuts, -0.22, 0.18)
    return jnp.clip(drawn, -limit, limit).astype(kind)


def setup_inputs(seed: int = 0) -> dict:
    splits = jax.random.split(jax.random.key(seed), 8)
    x_states = bell_draw(splits[0], (ORDER, S), 1.0, 6.0, ((0, 256),))
    h_blocks = bell_draw(splits[1], (NB, NNZ, BLK, BLK), (NNZ * BLK) ** -0.5, 0.15625, ((0, 256),))
    col_blocks = draw_col_blocks(jax.random.fold_in(splits[7], 71), 0)
    send_list = draw_send_list(jax.random.fold_in(splits[7], 71), 0)
    center = jnp.clip(jax.random.uniform(splits[4], (1,), jnp.float32, 0.2, 0.6), 0.2, 0.6)
    half_width = jnp.clip(jax.random.uniform(splits[5], (1,), jnp.float32, 1.0, 1.5), 1.0, 1.5)
    rotation = bell_draw(splits[6], (S, S), S ** -0.5, 0.125, ((0, 256),))
    return {"x_states": x_states, "h_blocks": h_blocks, "col_blocks": col_blocks, "send_list": send_list, "center": center, "half_width": half_width, "rotation": rotation}


def availability(col_blocks, send_list):
    total_blocks = col_blocks.shape[0]
    axis_count = total_blocks // B_DEV
    owner_device = col_blocks // B_DEV
    local_index = col_blocks - owner_device * B_DEV
    row_device = (jnp.arange(total_blocks, dtype=jnp.int32) // B_DEV)[:, None]
    offset = jnp.mod(row_device - owner_device + 2, axis_count) - 2
    list_slot = jnp.clip(jnp.where(offset > 0, offset - 1, 1 - offset), 0, 3).astype(jnp.int32)
    listed = send_list[owner_device, list_slot]
    is_listed = jnp.any(listed == local_index[..., None], axis=-1)
    return is_listed | (offset == 0)


def apply_matrix(masked, col_blocks, states):
    blocks = states.reshape(NB, BLK, S)

    def one_row(operands):
        row_blocks, columns = operands
        picked = blocks[columns].astype(jnp.float32)
        return jnp.einsum("kij,kjs->is", row_blocks.astype(jnp.float32), picked)

    return lax.map(one_row, (masked, col_blocks)).reshape(NB * BLK, S)


def reference(x_states, h_blocks, col_blocks, send_list, center, half_width, rotation):
    available = availability(col_blocks, send_list)
    masked = h_blocks * available[..., None, None].astype(jnp.bfloat16)
    center_value = center[0]
    half_value = half_width[0]
    x_wide = x_states.astype(jnp.float32)
    first_pass = ((apply_matrix(masked, col_blocks, x_states) - center_value * x_wide) / half_value).astype(jnp.bfloat16)
    second_term = apply_matrix(masked, col_blocks, first_pass) - center_value * first_pass.astype(jnp.float32)
    second_pass = (2.0 * second_term / half_value - x_wide).astype(jnp.bfloat16)
    return jnp.dot(second_pass, rotation, preferred_element_type=jnp.float32).astype(jnp.bfloat16)
```

```python
import functools

import jax
import jax.numpy as jnp
from jax import lax
from jax.experimental import pallas as pl
from jax.experimental.pallas import tpu as pltpu
from jax.sharding import PartitionSpec as P

BLK = 128
PAIR = 2 * BLK
WINDOW = 14 * BLK
WORK = 20 * 1024 * WINDOW
CHUNKS = (768, 256)
ANY = pl.BlockSpec(memory_space=pl.ANY)
HBM = pl.BlockSpec(memory_space=pltpu.HBM)
SMEM = pl.BlockSpec(memory_space=pltpu.SMEM)
VMEM = pl.BlockSpec(memory_space=pltpu.VMEM)


def call(kernel, name, outs, ins, args, scratch=(), aliases=None, flops=0):
    shapes = [jax.ShapeDtypeStruct(shape, jnp.bfloat16) for shape, _ in outs]
    return pl.pallas_call(
        kernel,
        out_shape=shapes,
        in_specs=ins,
        out_specs=[spec for _, spec in outs],
        scratch_shapes=scratch,
        input_output_aliases=aliases or {},
        compiler_params=pltpu.CompilerParams(vmem_limit_bytes=16 * 1024 * 1024),
        cost_estimate=pl.CostEstimate(flops=flops, transcendentals=0, bytes_accessed=0),
        name=name,
    )(*args)


def core_index():
    return lax.axis_index("rows") & 1


def pack_kernel(*refs):
    pieces, (mine_ref, other_ref, wide) = refs[:4], refs[4:]
    device = lax.axis_index("rows")
    ring = lax.shift_right_logical(device, 1) & 3
    width = mine_ref.shape[1]
    for i, piece in enumerate(pieces):
        place = ((ring - i) & 3) * 8
        wide[pl.ds(pl.multiple_of(place, 8), 8), :] = piece[...].astype(jnp.float32)
    for half, out in ((device & 1, mine_ref), (1 - (device & 1), other_ref)):
        columns = pl.ds(pl.multiple_of(half * width, BLK), width)
        out[...] = wide[:, columns].astype(out.dtype)


def pack(pieces):
    width = pieces[0].shape[1]
    outs = [((32, width // 2), VMEM)] * 2
    scratch = [pltpu.VMEM((32, width), jnp.float32)]
    return call(pack_kernel, "pack", outs, [VMEM] * 4, pieces, scratch)


def slab_kernel(mine_ref, got_ref, after_ref, out_ref, wide):
    core = core_index()
    for ref, side in ((mine_ref, core), (got_ref, 1 - core)):
        rows = ref[...].astype(jnp.float32)
        for i in range(4):
            place = pl.multiple_of(i * 16 + side * 8, 8)
            wide[pl.ds(place, 8), :] = rows[i * 8 : (i + 1) * 8, :]
    out_ref[...] = wide[...].astype(out_ref.dtype)


def slab(mine, got, after):
    shape = (64, mine.shape[1])
    scratch = [pltpu.VMEM(shape, jnp.float32)]
    ins = [VMEM, VMEM, ANY]
    return call(slab_kernel, "slab", [(shape, VMEM)], ins, (mine, got, after), scratch)[0]


def split_kernel(x_ref, out_ref, sem):
    width = out_ref.shape[1]
    columns = pl.ds(pl.multiple_of((1 - core_index()) * width, BLK), width)
    copy = pltpu.make_async_copy(x_ref.at[:, columns], out_ref, sem)
    copy.start()
    copy.wait()


def split(x_states):
    shape = (x_states.shape[0], x_states.shape[1] // 2)
    scratch = [pltpu.SemaphoreType.DMA]
    return call(split_kernel, "split", [(shape, VMEM)], [HBM], (x_states,), scratch)[0]


def tie_kernel(*refs):
    pass


def tie(array, *after):
    ins = [ANY] * (1 + len(after))
    return call(tie_kernel, "tie", [(array.shape, ANY)], ins, (array, *after), (), {0: 0})[0]


def assemble_kernel(chunks, x_ref, partner_ref, after_ref, *rest):
    outs, sems = rest[:-1], rest[-1]
    core = core_index()
    width = sum(chunks)

    def fill(mine):
        copies, at = [], 0
        for i, n in enumerate(chunks):
            columns = pl.ds(pl.multiple_of(core * width + at, BLK), n)
            up, dn = outs[2 * i], outs[2 * i + 1]
            if mine == 0:
                targets = ((0, 512, dn, 0), (256, 256, up, 0))
            else:
                targets = ((0, 256, dn, 512), (0, 512, up, 256))
            for j, (source, rows, out, place) in enumerate(targets):
                copy = pltpu.make_async_copy(
                    x_ref.at[pl.ds(source, rows), columns],
                    out.at[pl.ds(place, rows)],
                    sems.at[2 * i + j],
                )
                copy.start()
                copies.append(copy)
            at += n
        at = 0
        for i, n in enumerate(chunks):
            up, dn = outs[2 * i], outs[2 * i + 1]
            if mine == 0:
                dn[512:768, :] = partner_ref[0:256, at : at + n]
                up[256:768, :] = partner_ref[:, at : at + n]
            else:
                dn[0:512, :] = partner_ref[:, at : at + n]
                up[0:256, :] = partner_ref[256:512, at : at + n]
            at += n
        for copy in copies:
            copy.wait()

    @pl.when(core == 0)
    def _():
        fill(0)

    @pl.when(core == 1)
    def _():
        fill(1)


def assemble(x_states, partner, after, chunks):
    outs = [((768, n), VMEM) for n in chunks for _ in range(2)]
    scratch = [pltpu.SemaphoreType.DMA((2 * len(chunks),))]
    kernel = functools.partial(assemble_kernel, chunks)
    return call(kernel, "assemble", outs, [HBM, VMEM, ANY], (x_states, partner, after), scratch)


def build_kernel(device_count, col_ref, send_ref, h_ref, after_ref, out_ref):
    device = lax.axis_index("rows")
    out_ref[...] = jnp.zeros_like(out_ref)
    block_count = device_count * 4
    for row in range(4):
        band, half = row // 2, row % 2
        for k in range(12):
            column = col_ref[row, k]
            owner = lax.shift_right_logical(column, 2)
            local = column & 3
            offset = ((device - owner + 2) & (device_count - 1)) - 2
            slot = jnp.clip(jnp.where(offset > 0, offset - 1, 1 - offset), 0, 3)
            counts = offset == 0
            for j in range(4):
                counts = counts | (send_ref[slot, j, owner] == local)
            shift = ((column - (device * 4 + row) + 6) & (block_count - 1)) + half
            place = pl.ds(pl.multiple_of(shift * BLK, BLK), BLK)

            @pl.when(counts)
            def _(band=band, half=half, row=row, k=k, place=place):
                out_ref[band, half * BLK : (half + 1) * BLK, place] = h_ref[row, k]


def build(h_blocks, col_blocks, send_list, after, device_count):
    kernel = functools.partial(build_kernel, device_count)
    args = (col_blocks, send_list.transpose(1, 2, 0), h_blocks, after)
    return call(
        kernel, "build_bands", [((2, PAIR, WINDOW), VMEM)], [SMEM, SMEM, VMEM, ANY], args
    )[0]


def merge_kernel(own_ref, partner_ref, out_ref):
    core = core_index()
    out_ref[pl.ds(core * 2, 2)] = own_ref[...]
    out_ref[pl.ds(2 - core * 2, 2)] = partner_ref[...]


def merge(own, partner):
    outs = [((4, PAIR, WINDOW), VMEM)]
    return call(merge_kernel, "merge_bands", outs, [VMEM] * 2, (own, partner))[0]


def times_bands(g, bands, left, dn, up, right):
    edge = 768 - g * PAIR

    def dot(start, stop, states):
        return jnp.dot(bands[g, :, start:stop], states, preferred_element_type=jnp.float32)

    total = dot(edge, edge + 768, dn[...]) + dot(edge + 768, edge + 1024, up[512:768, :])
    if g < 3:
        total += dot(0, edge, left[g * PAIR :, :])
    if g > 0:
        total += dot(edge + 1024, WINDOW, right[: g * PAIR, :])
    return total


def own_rows(g, dn, up):
    rows = dn[g * PAIR : (g + 1) * PAIR, :] if g < 3 else up[512:768, :]
    return rows.astype(jnp.float32)


def first_kernel(center, half, bands, left, dn, up, right, after, out_up, out_dn):
    for g in range(4):
        total = times_bands(g, bands, left, dn, up, right)
        value = (total - center[0] * own_rows(g, dn, up)) / half[0]
        value = value.astype(jnp.bfloat16)
        if g < 3:
            out_dn[g * PAIR : (g + 1) * PAIR, :] = value
        if g > 0:
            out_up[(g - 1) * PAIR : g * PAIR, :] = value


def second_kernel(
    center, half, bands, left, dn, up, right, after, xdn, xup, out_mine, out_other, outs
):
    for g in range(4):
        total = times_bands(g, bands, left, dn, up, right)
        value = 2.0 * (total - center[0] * own_rows(g, dn, up)) / half[0] - own_rows(g, xdn, xup)
        outs[g * PAIR : (g + 1) * PAIR, :] = value.astype(jnp.bfloat16)
    core = core_index()
    out_mine[...] = outs[pl.ds(core * 512, 512), :]
    out_other[...] = outs[pl.ds(512 - core * 512, 512), :]


def first_pass(*args):
    n = args[4].shape[1]
    outs = [((768, n), VMEM)] * 2
    ins = [SMEM] * 2 + [VMEM] * 5 + [ANY]
    return call(first_kernel, "first_pass", outs, ins, args, flops=WORK * n)


def second_pass(*args):
    n = args[4].shape[1]
    outs = [((512, n), VMEM)] * 2
    ins = [SMEM] * 2 + [VMEM] * 5 + [ANY] + [VMEM] * 2
    scratch = [pltpu.VMEM((1024, n), jnp.bfloat16)]
    return call(second_kernel, "second_pass", outs, ins, args, scratch, flops=WORK * n)


def rotate_kernel(chunks, own_half, *refs):
    count = len(chunks)
    own, got, rot = refs[:count], refs[count : 2 * count], refs[2 * count]
    out_ref, outs, sems = refs[-3:]
    core = core_index()
    width = sum(chunks)
    tile = 256
    half = core if own_half else 1 - core
    stores = []
    for j in range(width // tile):
        columns = slice(j * tile, (j + 1) * tile)
        total, at = 0.0, 0
        for i, n in enumerate(chunks):
            for piece, side in ((own[i], core), (got[i], 1 - core)):
                rows = pl.ds(pl.multiple_of(side * width + at, BLK), n)
                total += jnp.dot(piece[...], rot[rows, columns], preferred_element_type=jnp.float32)
            at += n
        outs[:, columns] = total.astype(jnp.bfloat16)
        target = pl.ds(pl.multiple_of(half * width + j * tile, BLK), tile)
        stores.append(
            pltpu.make_async_copy(outs.at[:, columns], out_ref.at[:, target], sems.at[j])
        )
        stores[-1].start()
    for store in stores:
        store.wait()


def rotate(own, got, rot, chunks, out=None):
    width = sum(chunks)
    kernel = functools.partial(rotate_kernel, chunks, out is None)
    args, ins = [*own, *got, rot], [VMEM] * (2 * len(chunks) + 1)
    aliases = None
    if out is not None:
        aliases = {len(args): 0}
        args.append(out)
        ins.append(HBM)
    scratch = [pltpu.VMEM((512, width), jnp.bfloat16), pltpu.SemaphoreType.DMA((width // 256,))]
    return call(kernel, "rotate", [((512, 2 * width), HBM)], ins, args, scratch, aliases)[0]


def local(x_states, h_blocks, col_blocks, send_list, center, half_width, rotation):
    count = lax.axis_size("rows")
    swap = [(i, i ^ 1) for i in range(count)]
    onward = [(i, (i + 2) % count) for i in range(count)]
    backward = [(i, (i - 2) % count) for i in range(count)]

    def move(array, route):
        return lax.ppermute(array, "rows", route)

    def ring(step):
        return [(8 * (i // 8) + (i + 2 * step) % 8, i) for i in range(count)]

    plane = [[g * 8 + i for g in range(count // 8)] for i in range(8)]
    partner = move(split(x_states), swap)
    mine, other = pack([rotation] + [move(rotation, ring(step)) for step in (-1, -2, -3)])
    pieces = assemble(x_states, partner, mine, CHUNKS)
    ups, dns = pieces[0::2], pieces[1::2]
    lefts = [move(up, onward) for up in ups]
    rights = [move(dn, backward) for dn in dns]
    rows = slab(mine, move(other, swap), pieces[0])
    rot_own = lax.all_gather(rows, "rows", axis=0, tiled=True, axis_index_groups=plane)

    bands = build(h_blocks, col_blocks, send_list, rows, count)
    bands = merge(bands, move(bands, swap))
    fixed = (center, half_width, bands)

    firsts, after = [], mine
    for left, dn, up, right in zip(lefts, dns, ups, rights):
        up, dn = first_pass(*fixed, left, dn, up, right, after)
        after = up
        firsts.append((move(up, onward), dn, up, move(dn, backward)))
    own, got = [], []
    for first, xdn, xup in zip(firsts, dns, ups):
        mine, other = second_pass(*fixed, *first, after, xdn, xup)
        own.append(mine)
        got.append(move(other, swap))
        after = mine
    rot_own = tie(rot_own, *got)
    rot_got = move(rot_own, swap)
    out = rotate(own, got, rot_own, CHUNKS)
    return rotate(own, got, rot_got, CHUNKS, out)


def solution(mesh):
    placed = (
        P("rows", None),
        P("rows", None, None, None),
        P("rows", None),
        P(),
        P(),
        P(),
        P("rows", None),
    )
    return jax.shard_map(
        local, mesh=mesh, in_specs=placed, out_specs=P("rows", None), check_vma=False
    )
```

```python
import functools

import jax
import jax.numpy as jnp
from jax import lax
from jax.experimental import pallas as pl
from jax.experimental.pallas import tpu as pltpu
from jax.sharding import PartitionSpec as P

BLK = 128
PAIR = 2 * BLK
WINDOW = 14 * BLK
WORK = 20 * 1024 * WINDOW
CHUNKS = (512, 512)
EARLY = [(0, i) for i in range(4)] + [(1, i) for i in range(4)] + [(2, 0), (2, 1)]
LATE = [(2, 2), (2, 3)] + [(3, i) for i in range(4)]
ANY = pl.BlockSpec(memory_space=pl.ANY)
HBM = pl.BlockSpec(memory_space=pltpu.HBM)
SMEM = pl.BlockSpec(memory_space=pltpu.SMEM)
VMEM = pl.BlockSpec(memory_space=pltpu.VMEM)


def call(kernel, name, outs, ins, args, scratch=(), aliases=None, flops=0):
    shapes = [jax.ShapeDtypeStruct(shape, jnp.bfloat16) for shape, _ in outs]
    return pl.pallas_call(
        kernel,
        out_shape=shapes,
        in_specs=ins,
        out_specs=[spec for _, spec in outs],
        scratch_shapes=scratch,
        input_output_aliases=aliases or {},
        compiler_params=pltpu.CompilerParams(vmem_limit_bytes=16 * 1024 * 1024),
        cost_estimate=pl.CostEstimate(flops=flops, transcendentals=0, bytes_accessed=0),
        name=name,
    )(*args)


def core_index():
    return lax.axis_index("rows") & 1


def join_kernel(own_ref, got_ref, out_ref, wide):
    odd = (lax.axis_index("rows") >> 3) & 1
    wide[pl.ds(pl.multiple_of(odd * 8, 8), 8), :] = own_ref[...].astype(jnp.float32)
    wide[pl.ds(pl.multiple_of(8 - odd * 8, 8), 8), :] = got_ref[...].astype(jnp.float32)
    out_ref[...] = wide[...].astype(out_ref.dtype)


def join(own, got):
    shape = (16, own.shape[1])
    scratch = [pltpu.VMEM(shape, jnp.float32)]
    return call(join_kernel, "join", [(shape, VMEM)], [VMEM] * 2, (own, got), scratch)[0]


def pack_kernel(*refs):
    pieces, (mine_ref, other_ref, wide) = refs[:4], refs[4:]
    device = lax.axis_index("rows")
    ring = (device >> 1) & 3
    width = mine_ref.shape[1]
    for i, piece in enumerate(pieces):
        rows = piece[...].astype(jnp.float32)
        for j in range(2):
            place = pl.multiple_of(j * 32 + ((ring - i) & 3) * 8, 8)
            wide[pl.ds(place, 8), :] = rows[j * 8 : (j + 1) * 8, :]
    for half, out in ((device & 1, mine_ref), (1 - (device & 1), other_ref)):
        columns = pl.ds(pl.multiple_of(half * width, BLK), width)
        out[...] = wide[:, columns].astype(out.dtype)


def pack(pieces):
    width = pieces[0].shape[1]
    outs = [((64, width // 2), VMEM)] * 2
    scratch = [pltpu.VMEM((64, width), jnp.float32)]
    return call(pack_kernel, "pack", outs, [VMEM] * 4, pieces, scratch)


def slab_kernel(mine_ref, got_ref, after_ref, out_ref, wide):
    core = core_index()
    for ref, side in ((mine_ref, core), (got_ref, 1 - core)):
        rows = ref[...].astype(jnp.float32)
        for i in range(8):
            place = pl.multiple_of(i * 16 + side * 8, 8)
            wide[pl.ds(place, 8), :] = rows[i * 8 : (i + 1) * 8, :]
    out_ref[...] = wide[...].astype(out_ref.dtype)


def slab(mine, got, after):
    shape = (128, mine.shape[1])
    scratch = [pltpu.VMEM(shape, jnp.float32)]
    ins = [VMEM, VMEM, ANY]
    return call(slab_kernel, "slab", [(shape, VMEM)], ins, (mine, got, after), scratch)[0]


def split_kernel(x_ref, out_ref, sem):
    width = out_ref.shape[1]
    columns = pl.ds(pl.multiple_of((1 - core_index()) * width, BLK), width)
    copy = pltpu.make_async_copy(x_ref.at[:, columns], out_ref, sem)
    copy.start()
    copy.wait()


def split(x_states):
    shape = (x_states.shape[0], x_states.shape[1] // 2)
    scratch = [pltpu.SemaphoreType.DMA]
    return call(split_kernel, "split", [(shape, VMEM)], [HBM], (x_states,), scratch)[0]


def assemble_kernel(chunks, x_ref, partner_ref, after_ref, *rest):
    outs, sems = rest[:-1], rest[-1]
    core = core_index()
    width = sum(chunks)

    def fill(mine):
        copies, at = [], 0
        for i, n in enumerate(chunks):
            columns = pl.ds(pl.multiple_of(core * width + at, BLK), n)
            up, dn = outs[2 * i], outs[2 * i + 1]
            if mine == 0:
                targets = ((0, 512, dn, 0), (256, 256, up, 0))
            else:
                targets = ((0, 256, dn, 512), (0, 512, up, 256))
            for j, (source, rows, out, place) in enumerate(targets):
                copy = pltpu.make_async_copy(
                    x_ref.at[pl.ds(source, rows), columns],
                    out.at[pl.ds(place, rows)],
                    sems.at[2 * i + j],
                )
                copy.start()
                copies.append(copy)
            at += n
        at = 0
        for i, n in enumerate(chunks):
            up, dn = outs[2 * i], outs[2 * i + 1]
            if mine == 0:
                dn[512:768, :] = partner_ref[0:256, at : at + n]
                up[256:768, :] = partner_ref[:, at : at + n]
            else:
                dn[0:512, :] = partner_ref[:, at : at + n]
                up[0:256, :] = partner_ref[256:512, at : at + n]
            at += n
        for copy in copies:
            copy.wait()

    @pl.when(core == 0)
    def _():
        fill(0)

    @pl.when(core == 1)
    def _():
        fill(1)


def assemble(x_states, partner, after, chunks):
    outs = [((768, n), VMEM) for n in chunks for _ in range(2)]
    scratch = [pltpu.SemaphoreType.DMA((2 * len(chunks),))]
    kernel = functools.partial(assemble_kernel, chunks)
    return call(kernel, "assemble", outs, [HBM, VMEM, ANY], (x_states, partner, after), scratch)


def build_kernel(device_count, col_ref, send_ref, h_ref, after_ref, *out_refs):
    device = lax.axis_index("rows")
    for out_ref in out_refs:
        out_ref[...] = jnp.zeros_like(out_ref)
    block_count = device_count * 4
    for row in range(4):
        band, half = row // 2, row % 2
        for k in range(12):
            column = col_ref[row, k]
            owner = lax.shift_right_logical(column, 2)
            local = column & 3
            offset = ((device - owner + 2) & (device_count - 1)) - 2
            slot = jnp.clip(jnp.where(offset > 0, offset - 1, 1 - offset), 0, 3)
            counts = offset == 0
            for j in range(4):
                counts = counts | (send_ref[slot, j, owner] == local)
            shift = ((column - (device * 4 + row) + 6) & (block_count - 1)) + half
            place = pl.ds(pl.multiple_of(shift * BLK, BLK), BLK)

            @pl.when(counts)
            def _(out_ref=out_refs[band], half=half, row=row, k=k, place=place):
                out_ref[half * BLK : (half + 1) * BLK, place] = h_ref[row, k]


def build(h_blocks, col_blocks, send_list, after, device_count):
    kernel = functools.partial(build_kernel, device_count)
    args = (col_blocks, send_list.transpose(1, 2, 0), h_blocks, after)
    outs = [((PAIR, WINDOW), VMEM)] * 2
    return call(kernel, "build_bands", outs, [SMEM, SMEM, VMEM, ANY], args)


def merge_kernel(*refs):
    out_ref = refs[-1]
    core = core_index()
    for i in range(2):
        out_ref[core * 2 + i] = refs[i][...]
        out_ref[2 - core * 2 + i] = refs[2 + i][...]


def merge(own, partner):
    outs = [((4, PAIR, WINDOW), VMEM)]
    return call(merge_kernel, "merge_bands", outs, [VMEM] * 4, (*own, *partner))[0]


def times_bands(g, columns, bands, left, dn, up, right):
    edge = 768 - g * PAIR

    def dot(start, stop, states):
        return jnp.dot(bands[g, :, start:stop], states, preferred_element_type=jnp.float32)

    total = dot(edge, edge + 768, dn[:, columns])
    total += dot(edge + 768, edge + 1024, up[512:768, columns])
    if g < 3:
        total += dot(0, edge, left[g * PAIR :, columns])
    if g > 0:
        total += dot(edge + 1024, WINDOW, right[: g * PAIR, columns])
    return total


def own_rows(g, columns, dn, up):
    rows = dn[g * PAIR : (g + 1) * PAIR, columns] if g < 3 else up[512:768, columns]
    return rows.astype(jnp.float32)


def first_kernel(columns, center, half, bands, left, dn, up, right, *rest):
    out_up, out_dn = rest[-2:]
    for g in range(4):
        total = times_bands(g, columns, bands, left, dn, up, right)
        value = (total - center[0] * own_rows(g, columns, dn, up)) / half[0]
        value = value.astype(jnp.bfloat16)
        if g < 3:
            out_dn[g * PAIR : (g + 1) * PAIR, :] = value
        if g > 0:
            out_up[(g - 1) * PAIR : g * PAIR, :] = value


def second_kernel(
    columns, center, half, bands, left, dn, up, right, after, xdn, xup, out_mine, out_other, outs
):
    for g in range(4):
        total = times_bands(g, columns, bands, left, dn, up, right)
        value = 2.0 * (total - center[0] * own_rows(g, columns, dn, up)) / half[0]
        value -= own_rows(g, columns, xdn, xup)
        outs[g * PAIR : (g + 1) * PAIR, :] = value.astype(jnp.bfloat16)
    core = core_index()
    out_mine[...] = outs[pl.ds(core * 512, 512), :]
    out_other[...] = outs[pl.ds(512 - core * 512, 512), :]


def first_pass(columns, *args):
    n = columns.stop - columns.start
    outs = [((768, n), VMEM)] * 2
    ins = [SMEM] * 2 + [VMEM] * 5 + [ANY] * (len(args) - 7)
    kernel = functools.partial(first_kernel, columns)
    return call(kernel, "first_pass", outs, ins, args, flops=WORK * n // 20)


def second_pass(columns, *args):
    n = columns.stop - columns.start
    outs = [((512, n), VMEM)] * 2
    ins = [SMEM] * 2 + [VMEM] * 5 + [ANY] + [VMEM] * 2
    scratch = [pltpu.VMEM((1024, n), jnp.bfloat16)]
    kernel = functools.partial(second_kernel, columns)
    return call(kernel, "second_pass", outs, ins, args, scratch, flops=WORK * n)


def tie_kernel(*refs):
    pass


def tie(array, after):
    return call(tie_kernel, "tie", [(array.shape, ANY)], [ANY] * 2, (array, after), (), {0: 0})[0]


def stack_kernel(count, *refs):
    out, at = refs[-1], 0
    for ref in refs[:count]:
        out[at : at + ref.shape[0], :] = ref[...]
        at += ref.shape[0]


def stack(pieces, *after):
    shape = (sum(piece.shape[0] for piece in pieces), pieces[0].shape[1])
    kernel = functools.partial(stack_kernel, len(pieces))
    ins = [VMEM] * len(pieces) + [ANY] * len(after)
    return call(kernel, "stack", [(shape, VMEM)], ins, (*pieces, *after))[0]


def z_step(y):
    return 1 if y < 2 else -1


def x_step(y, z, z_count, forward):
    if forward:
        return -1 if (y == 3 and z == 0) else 1
    return 1 if (y == 0 and z == z_count - 1) else -1


def rotate_kernel(chunks, own_half, *refs):
    count = len(chunks)
    own, got, parts = refs[:count], refs[count : 2 * count], refs[2 * count : 2 * count + 2]
    out_ref, rot, outs, sems = refs[-4:]
    device = lax.axis_index("rows")
    core, y = device & 1, (device >> 1) & 3
    z, x = (device >> 3) & 7, device >> 6
    z_way = jnp.where(y < 2, 1, -1)
    ways = (
        jnp.where((y == 3) & (z == 0), -1, 1),
        jnp.where((y == 0) & (z == 7), 1, -1),
    )
    for part, pieces in zip(parts, (EARLY, LATE)):
        for at, (j, i) in enumerate(pieces):
            from_x = (x - ways[j % 2] * i) & 3
            from_z = ((z >> 1) - z_way * j) & 3
            place = pl.multiple_of(from_x * 512 + from_z * 128, 128)
            rot[pl.ds(place, 128), :] = part[at * 128 : (at + 1) * 128, :]
    width = sum(chunks)
    tile = 256
    half = core if own_half else 1 - core
    stores = []
    for t in range(width // tile):
        columns = slice(t * tile, (t + 1) * tile)
        total, at = 0.0, 0
        for i, n in enumerate(chunks):
            for piece, side in ((own[i], core), (got[i], 1 - core)):
                rows = pl.ds(pl.multiple_of(side * width + at, BLK), n)
                total += jnp.dot(piece[...], rot[rows, columns], preferred_element_type=jnp.float32)
            at += n
        outs[:, columns] = total.astype(jnp.bfloat16)
        target = pl.ds(pl.multiple_of(half * width + t * tile, BLK), tile)
        stores.append(
            pltpu.make_async_copy(outs.at[:, columns], out_ref.at[:, target], sems.at[t])
        )
        stores[-1].start()
    for store in stores:
        store.wait()


def rotate(own, got, parts, chunks, out=None):
    width = sum(chunks)
    kernel = functools.partial(rotate_kernel, chunks, out is None)
    args, ins = [*own, *got, *parts], [VMEM] * (2 * len(chunks) + 2)
    aliases = None
    if out is not None:
        aliases = {len(args): 0}
        args.append(out)
        ins.append(HBM)
    scratch = [
        pltpu.VMEM((2 * width, width), jnp.bfloat16),
        pltpu.VMEM((512, width), jnp.bfloat16),
        pltpu.SemaphoreType.DMA((width // 256,)),
    ]
    return call(kernel, "rotate", [((512, 2 * width), HBM)], ins, args, scratch, aliases)[0]


def local(x_states, h_blocks, col_blocks, send_list, center, half_width, rotation):
    count = lax.axis_size("rows")
    swap = [(i, i ^ 1) for i in range(count)]
    onward = [(i, (i + 2) % count) for i in range(count)]
    backward = [(i, (i - 2) % count) for i in range(count)]

    def move(array, route):
        return lax.ppermute(array, "rows", route)

    def ring(step):
        return [(8 * (i // 8) + (i + 2 * step) % 8, i) for i in range(count)]

    def place(i):
        return i >> 6, (i >> 3) & 7, (i >> 1) & 3

    def along_z(i):
        x, z, y = place(i)
        return x * 64 + (z + 2 * z_step(y)) % 8 * 8 + i % 8

    def along_x(i, forward):
        x, z, y = place(i)
        return (x + x_step(y, z, 8, forward)) % 4 * 64 + i % 64

    z_route = [(i, along_z(i)) for i in range(count)]
    x_routes = [[(i, along_x(i, forward)) for i in range(count)] for forward in (True, False)]

    partner = move(split(x_states), swap)
    rotation = join(rotation, move(rotation, [(i, i ^ 8) for i in range(count)]))
    mine, other = pack([rotation] + [move(rotation, ring(step)) for step in (-1, -2, -3)])
    up, dn = assemble(x_states, partner, mine, (sum(CHUNKS),))
    left, right = move(up, onward), move(dn, backward)
    rows = slab(mine, move(other, swap), up)
    bands = build(h_blocks, col_blocks, send_list, rows, count)
    bands = merge(bands, [move(band, swap) for band in bands])
    slabs = [rows, tie(move(rows, z_route), bands)]
    slabs.append(move(slabs[1], z_route))
    chains = [[stack([rows], bands)], [slabs[1]], [slabs[2]]]

    def on(j, steps):
        for _ in range(steps):
            chains[j].append(move(chains[j][-1], x_routes[j % 2]))

    on(0, 3)
    on(1, 2)

    fixed = (center, half_width, bands)

    starts = [sum(CHUNKS[:i]) for i in range(len(CHUNKS))]
    columns = [slice(start, start + n) for start, n in zip(starts, CHUNKS)]
    every = slice(0, sum(CHUNKS))
    first_up, first_dn = first_pass(every, *fixed, left, dn, up, right, slabs[2], chains[0][3], chains[1][2])
    halo = (move(first_up, onward), first_dn, first_up, move(first_dn, backward))
    after = first_up
    chains[1][2], chains[2][0] = tie(chains[1][2], after), tie(chains[2][0], after)
    chains.append([move(chains[2][0], z_route)])
    on(1, 1)
    on(2, 3)
    on(3, 3)
    own, got = [], []
    for part in columns:
        mine, other = second_pass(part, *fixed, *halo, after, dn, up)
        after = mine
        own.append(mine)
        got.append(move(other, swap))
    parts = [
        stack([chains[j][i] for j, i in EARLY]),
        stack([chains[j][i] for j, i in LATE]),
    ]
    out = rotate(own, got, parts, CHUNKS)
    return rotate(own, got, [move(part, swap) for part in parts], CHUNKS, out)


def solution(mesh):
    placed = (
        P("rows", None),
        P("rows", None, None, None),
        P("rows", None),
        P(),
        P(),
        P(),
        P("rows", None),
    )
    return jax.shard_map(
        local, mesh=mesh, in_specs=placed, out_specs=P("rows", None), check_vma=False
    )
```

```python
import functools

import jax
import jax.numpy as jnp
from jax import lax
from jax.experimental import pallas as pl
from jax.experimental.pallas import tpu as pltpu
from jax.sharding import PartitionSpec as P

BLK = 128
PAIR = 2 * BLK
WINDOW = 14 * BLK
WORK = 20 * 1024 * WINDOW
CHUNKS = (512, 512)
EARLY = [(0, i) for i in range(4)] + [(1, i) for i in range(4)] + [(2, 0), (2, 1)]
LATE = [(2, 2), (2, 3)] + [(3, i) for i in range(4)]
ANY = pl.BlockSpec(memory_space=pl.ANY)
HBM = pl.BlockSpec(memory_space=pltpu.HBM)
SMEM = pl.BlockSpec(memory_space=pltpu.SMEM)
VMEM = pl.BlockSpec(memory_space=pltpu.VMEM)


def call(kernel, name, outs, ins, args, scratch=(), aliases=None, flops=0):
    shapes = [jax.ShapeDtypeStruct(shape, jnp.bfloat16) for shape, _ in outs]
    return pl.pallas_call(
        kernel,
        out_shape=shapes,
        in_specs=ins,
        out_specs=[spec for _, spec in outs],
        scratch_shapes=scratch,
        input_output_aliases=aliases or {},
        compiler_params=pltpu.CompilerParams(vmem_limit_bytes=16 * 1024 * 1024),
        cost_estimate=pl.CostEstimate(flops=flops, transcendentals=0, bytes_accessed=0),
        name=name,
    )(*args)


def core_index():
    return lax.axis_index("rows") & 1


def join_kernel(own_ref, got_ref, out_ref, wide):
    odd = (lax.axis_index("rows") >> 3) & 1
    wide[pl.ds(pl.multiple_of(odd * 8, 8), 8), :] = own_ref[...].astype(jnp.float32)
    wide[pl.ds(pl.multiple_of(8 - odd * 8, 8), 8), :] = got_ref[...].astype(jnp.float32)
    out_ref[...] = wide[...].astype(out_ref.dtype)


def join(own, got):
    shape = (16, own.shape[1])
    scratch = [pltpu.VMEM(shape, jnp.float32)]
    return call(join_kernel, "join", [(shape, VMEM)], [VMEM] * 2, (own, got), scratch)[0]


def pack_kernel(*refs):
    pieces, (mine_ref, other_ref, wide) = refs[:4], refs[4:]
    device = lax.axis_index("rows")
    ring = (device >> 1) & 3
    width = mine_ref.shape[1]
    for i, piece in enumerate(pieces):
        rows = piece[...].astype(jnp.float32)
        for j in range(2):
            place = pl.multiple_of(j * 32 + ((ring - i) & 3) * 8, 8)
            wide[pl.ds(place, 8), :] = rows[j * 8 : (j + 1) * 8, :]
    for half, out in ((device & 1, mine_ref), (1 - (device & 1), other_ref)):
        columns = pl.ds(pl.multiple_of(half * width, BLK), width)
        out[...] = wide[:, columns].astype(out.dtype)


def pack(pieces):
    width = pieces[0].shape[1]
    outs = [((64, width // 2), VMEM)] * 2
    scratch = [pltpu.VMEM((64, width), jnp.float32)]
    return call(pack_kernel, "pack", outs, [VMEM] * 4, pieces, scratch)


def slab_kernel(mine_ref, got_ref, after_ref, out_ref, wide):
    core = core_index()
    for ref, side in ((mine_ref, core), (got_ref, 1 - core)):
        rows = ref[...].astype(jnp.float32)
        for i in range(8):
            place = pl.multiple_of(i * 16 + side * 8, 8)
            wide[pl.ds(place, 8), :] = rows[i * 8 : (i + 1) * 8, :]
    out_ref[...] = wide[...].astype(out_ref.dtype)


def slab(mine, got, after):
    shape = (128, mine.shape[1])
    scratch = [pltpu.VMEM(shape, jnp.float32)]
    ins = [VMEM, VMEM, ANY]
    return call(slab_kernel, "slab", [(shape, VMEM)], ins, (mine, got, after), scratch)[0]


def split_kernel(x_ref, out_ref, sem):
    width = out_ref.shape[1]
    columns = pl.ds(pl.multiple_of((1 - core_index()) * width, BLK), width)
    copy = pltpu.make_async_copy(x_ref.at[:, columns], out_ref, sem)
    copy.start()
    copy.wait()


def split(x_states):
    shape = (x_states.shape[0], x_states.shape[1] // 2)
    scratch = [pltpu.SemaphoreType.DMA]
    return call(split_kernel, "split", [(shape, VMEM)], [HBM], (x_states,), scratch)[0]


def assemble_kernel(chunks, x_ref, partner_ref, after_ref, *rest):
    outs, sems = rest[:-1], rest[-1]
    core = core_index()
    width = sum(chunks)

    def fill(mine):
        copies, at = [], 0
        for i, n in enumerate(chunks):
            columns = pl.ds(pl.multiple_of(core * width + at, BLK), n)
            up, dn = outs[2 * i], outs[2 * i + 1]
            if mine == 0:
                targets = ((0, 512, dn, 0), (256, 256, up, 0))
            else:
                targets = ((0, 256, dn, 512), (0, 512, up, 256))
            for j, (source, rows, out, place) in enumerate(targets):
                copy = pltpu.make_async_copy(
                    x_ref.at[pl.ds(source, rows), columns],
                    out.at[pl.ds(place, rows)],
                    sems.at[2 * i + j],
                )
                copy.start()
                copies.append(copy)
            at += n
        at = 0
        for i, n in enumerate(chunks):
            up, dn = outs[2 * i], outs[2 * i + 1]
            if mine == 0:
                dn[512:768, :] = partner_ref[0:256, at : at + n]
                up[256:768, :] = partner_ref[:, at : at + n]
            else:
                dn[0:512, :] = partner_ref[:, at : at + n]
                up[0:256, :] = partner_ref[256:512, at : at + n]
            at += n
        for copy in copies:
            copy.wait()

    @pl.when(core == 0)
    def _():
        fill(0)

    @pl.when(core == 1)
    def _():
        fill(1)


def assemble(x_states, partner, after, chunks):
    outs = [((768, n), VMEM) for n in chunks for _ in range(2)]
    scratch = [pltpu.SemaphoreType.DMA((2 * len(chunks),))]
    kernel = functools.partial(assemble_kernel, chunks)
    return call(kernel, "assemble", outs, [HBM, VMEM, ANY], (x_states, partner, after), scratch)


def build_kernel(device_count, col_ref, send_ref, h_ref, after_ref, *out_refs):
    device = lax.axis_index("rows")
    for out_ref in out_refs:
        out_ref[...] = jnp.zeros_like(out_ref)
    block_count = device_count * 4
    for row in range(4):
        band, half = row // 2, row % 2
        for k in range(12):
            column = col_ref[row, k]
            owner = lax.shift_right_logical(column, 2)
            local = column & 3
            offset = ((device - owner + 2) & (device_count - 1)) - 2
            slot = jnp.clip(jnp.where(offset > 0, offset - 1, 1 - offset), 0, 3)
            counts = offset == 0
            for j in range(4):
                counts = counts | (send_ref[slot, j, owner] == local)
            shift = ((column - (device * 4 + row) + 6) & (block_count - 1)) + half
            place = pl.ds(pl.multiple_of(shift * BLK, BLK), BLK)

            @pl.when(counts)
            def _(out_ref=out_refs[band], half=half, row=row, k=k, place=place):
                out_ref[half * BLK : (half + 1) * BLK, place] = h_ref[row, k]


def build(h_blocks, col_blocks, send_list, after, device_count):
    kernel = functools.partial(build_kernel, device_count)
    args = (col_blocks, send_list.transpose(1, 2, 0), h_blocks, after)
    outs = [((PAIR, WINDOW), VMEM)] * 2
    return call(kernel, "build_bands", outs, [SMEM, SMEM, VMEM, ANY], args)


def merge_kernel(*refs):
    out_ref = refs[-1]
    core = core_index()
    for i in range(2):
        out_ref[core * 2 + i] = refs[i][...]
        out_ref[2 - core * 2 + i] = refs[2 + i][...]


def merge(own, partner):
    outs = [((4, PAIR, WINDOW), VMEM)]
    return call(merge_kernel, "merge_bands", outs, [VMEM] * 4, (*own, *partner))[0]


def times_bands(g, columns, bands, left, dn, up, right):
    edge = 768 - g * PAIR

    def dot(start, stop, states):
        return jnp.dot(bands[g, :, start:stop], states, preferred_element_type=jnp.float32)

    total = dot(edge, edge + 768, dn[:, columns])
    total += dot(edge + 768, edge + 1024, up[512:768, columns])
    if g < 3:
        total += dot(0, edge, left[g * PAIR :, columns])
    if g > 0:
        total += dot(edge + 1024, WINDOW, right[: g * PAIR, columns])
    return total


def own_rows(g, columns, dn, up):
    rows = dn[g * PAIR : (g + 1) * PAIR, columns] if g < 3 else up[512:768, columns]
    return rows.astype(jnp.float32)


def first_kernel(columns, center, half, bands, left, dn, up, right, *rest):
    out_up, out_dn = rest[-2:]
    for g in range(4):
        total = times_bands(g, columns, bands, left, dn, up, right)
        value = (total - center[0] * own_rows(g, columns, dn, up)) / half[0]
        value = value.astype(jnp.bfloat16)
        if g < 3:
            out_dn[g * PAIR : (g + 1) * PAIR, :] = value
        if g > 0:
            out_up[(g - 1) * PAIR : g * PAIR, :] = value


def second_kernel(
    columns, center, half, bands, left, dn, up, right, after, xdn, xup, out_mine, out_other, outs
):
    for g in range(4):
        total = times_bands(g, columns, bands, left, dn, up, right)
        value = 2.0 * (total - center[0] * own_rows(g, columns, dn, up)) / half[0]
        value -= own_rows(g, columns, xdn, xup)
        outs[g * PAIR : (g + 1) * PAIR, :] = value.astype(jnp.bfloat16)
    core = core_index()
    out_mine[...] = outs[pl.ds(core * 512, 512), :]
    out_other[...] = outs[pl.ds(512 - core * 512, 512), :]


def first_pass(columns, *args):
    n = columns.stop - columns.start
    outs = [((768, n), VMEM)] * 2
    ins = [SMEM] * 2 + [VMEM] * 5 + [ANY] * (len(args) - 7)
    kernel = functools.partial(first_kernel, columns)
    return call(kernel, "first_pass", outs, ins, args, flops=WORK * n // 20)


def second_pass(columns, *args):
    n = columns.stop - columns.start
    outs = [((512, n), VMEM)] * 2
    ins = [SMEM] * 2 + [VMEM] * 5 + [ANY] + [VMEM] * 2
    scratch = [pltpu.VMEM((1024, n), jnp.bfloat16)]
    kernel = functools.partial(second_kernel, columns)
    return call(kernel, "second_pass", outs, ins, args, scratch, flops=WORK * n)


def tie_kernel(*refs):
    pass


def tie(array, after):
    return call(tie_kernel, "tie", [(array.shape, ANY)], [ANY] * 2, (array, after), (), {0: 0})[0]


def stack_kernel(count, *refs):
    out, at = refs[-1], 0
    for ref in refs[:count]:
        out[at : at + ref.shape[0], :] = ref[...]
        at += ref.shape[0]


def stack(pieces, *after):
    shape = (sum(piece.shape[0] for piece in pieces), pieces[0].shape[1])
    kernel = functools.partial(stack_kernel, len(pieces))
    ins = [VMEM] * len(pieces) + [ANY] * len(after)
    return call(kernel, "stack", [(shape, VMEM)], ins, (*pieces, *after))[0]


def z_step(y):
    return 1 if y < 2 else -1


def x_step(y, z, z_count, forward):
    if forward:
        return -1 if (y == 3 and z == 0) else 1
    return 1 if (y == 0 and z == z_count - 1) else -1


def rotate_kernel(chunks, own_half, *refs):
    count = len(chunks)
    own, got, parts = refs[:count], refs[count : 2 * count], refs[2 * count : 2 * count + 2]
    out_ref, rot, outs, sems = refs[-4:]
    device = lax.axis_index("rows")
    core, y = device & 1, (device >> 1) & 3
    z, x = (device >> 3) & 7, device >> 6
    z_way = jnp.where(y < 2, 1, -1)
    ways = (
        jnp.where((y == 3) & (z == 0), -1, 1),
        jnp.where((y == 0) & (z == 7), 1, -1),
    )
    for part, pieces in zip(parts, (EARLY, LATE)):
        for at, (j, i) in enumerate(pieces):
            from_x = (x - ways[j % 2] * i) & 3
            from_z = ((z >> 1) - z_way * j) & 3
            place = pl.multiple_of(from_x * 512 + from_z * 128, 128)
            rot[pl.ds(place, 128), :] = part[at * 128 : (at + 1) * 128, :]
    width = sum(chunks)
    tile = 256
    half = core if own_half else 1 - core
    stores = []
    for t in range(width // tile):
        columns = slice(t * tile, (t + 1) * tile)
        total, at = 0.0, 0
        for i, n in enumerate(chunks):
            for piece, side in ((own[i], core), (got[i], 1 - core)):
                rows = pl.ds(pl.multiple_of(side * width + at, BLK), n)
                total += jnp.dot(piece[...], rot[rows, columns], preferred_element_type=jnp.float32)
            at += n
        outs[:, columns] = total.astype(jnp.bfloat16)
        target = pl.ds(pl.multiple_of(half * width + t * tile, BLK), tile)
        stores.append(
            pltpu.make_async_copy(outs.at[:, columns], out_ref.at[:, target], sems.at[t])
        )
        stores[-1].start()
    for store in stores:
        store.wait()


def rotate(own, got, parts, chunks, out=None):
    width = sum(chunks)
    kernel = functools.partial(rotate_kernel, chunks, out is None)
    args, ins = [*own, *got, *parts], [VMEM] * (2 * len(chunks) + 2)
    aliases = None
    if out is not None:
        aliases = {len(args): 0}
        args.append(out)
        ins.append(HBM)
    scratch = [
        pltpu.VMEM((2 * width, width), jnp.bfloat16),
        pltpu.VMEM((512, width), jnp.bfloat16),
        pltpu.SemaphoreType.DMA((width // 256,)),
    ]
    return call(kernel, "rotate", [((512, 2 * width), HBM)], ins, args, scratch, aliases)[0]


def local(x_states, h_blocks, col_blocks, send_list, center, half_width, rotation):
    count = lax.axis_size("rows")
    swap = [(i, i ^ 1) for i in range(count)]
    onward = [(i, (i + 2) % count) for i in range(count)]
    backward = [(i, (i - 2) % count) for i in range(count)]

    def move(array, route):
        return lax.ppermute(array, "rows", route)

    def ring(step):
        return [(8 * (i // 8) + (i + 2 * step) % 8, i) for i in range(count)]

    def place(i):
        return i >> 6, (i >> 3) & 7, (i >> 1) & 3

    def along_z(i):
        x, z, y = place(i)
        return x * 64 + (z + 2 * z_step(y)) % 8 * 8 + i % 8

    def along_x(i, forward):
        x, z, y = place(i)
        return (x + x_step(y, z, 8, forward)) % 4 * 64 + i % 64

    z_route = [(i, along_z(i)) for i in range(count)]
    x_routes = [[(i, along_x(i, forward)) for i in range(count)] for forward in (True, False)]

    partner = move(split(x_states), swap)
    rotation = join(rotation, move(rotation, [(i, i ^ 8) for i in range(count)]))
    mine, other = pack([rotation] + [move(rotation, ring(step)) for step in (-1, -2, -3)])
    up, dn = assemble(x_states, partner, mine, (sum(CHUNKS),))
    left, right = move(up, onward), move(dn, backward)
    rows = slab(mine, move(other, swap), up)
    bands = build(h_blocks, col_blocks, send_list, rows, count)
    bands = merge(bands, [move(band, swap) for band in bands])
    slabs = [rows, tie(move(rows, z_route), bands)]
    slabs.append(move(slabs[1], z_route))
    chains = [[stack([rows], bands)], [slabs[1]], [slabs[2]]]

    def on(j, steps):
        for _ in range(steps):
            chains[j].append(move(chains[j][-1], x_routes[j % 2]))

    on(0, 3)
    on(1, 2)

    fixed = (center, half_width, bands)

    starts = [sum(CHUNKS[:i]) for i in range(len(CHUNKS))]
    columns = [slice(start, start + n) for start, n in zip(starts, CHUNKS)]
    every = slice(0, sum(CHUNKS))
    first_up, first_dn = first_pass(every, *fixed, left, dn, up, right, slabs[2], chains[0][3], chains[1][2])
    halo = (move(first_up, onward), first_dn, first_up, move(first_dn, backward))
    after = first_up
    chains[1][2], chains[2][0] = tie(chains[1][2], after), tie(chains[2][0], after)
    chains.append([move(chains[2][0], z_route)])
    on(1, 1)
    on(2, 3)
    on(3, 3)
    own, got = [], []
    for part in columns:
        mine, other = second_pass(part, *fixed, *halo, after, dn, up)
        after = mine
        own.append(mine)
        got.append(move(other, swap))
    parts = [
        stack([chains[j][i] for j, i in EARLY]),
        stack([chains[j][i] for j, i in LATE], own[-1]),
    ]
    out = rotate(own, got, parts, CHUNKS)
    return rotate(own, got, [move(part, swap) for part in parts], CHUNKS, out)


def solution(mesh):
    placed = (
        P("rows", None),
        P("rows", None, None, None),
        P("rows", None),
        P(),
        P(),
        P(),
        P("rows", None),
    )
    return jax.shard_map(
        local, mesh=mesh, in_specs=placed, out_specs=P("rows", None), check_vma=False
    )
```

```python
import functools

import jax
import jax.numpy as jnp
from jax import lax
from jax.experimental import pallas as pl
from jax.experimental.pallas import tpu as pltpu
from jax.sharding import PartitionSpec as P

BLK = 128
PAIR = 2 * BLK
WINDOW = 14 * BLK
WORK = 20 * 1024 * WINDOW
CHUNKS = (512, 512)
EARLY = [(0, i) for i in range(4)] + [(1, i) for i in range(4)] + [(2, i) for i in range(3)] + [(3, 0), (3, 1)]
LATE = [(2, 3), (3, 2), (3, 3)]
ANY = pl.BlockSpec(memory_space=pl.ANY)
HBM = pl.BlockSpec(memory_space=pltpu.HBM)
SMEM = pl.BlockSpec(memory_space=pltpu.SMEM)
VMEM = pl.BlockSpec(memory_space=pltpu.VMEM)


def call(kernel, name, outs, ins, args, scratch=(), aliases=None, flops=0):
    shapes = [jax.ShapeDtypeStruct(shape, jnp.bfloat16) for shape, _ in outs]
    return pl.pallas_call(
        kernel,
        out_shape=shapes,
        in_specs=ins,
        out_specs=[spec for _, spec in outs],
        scratch_shapes=scratch,
        input_output_aliases=aliases or {},
        compiler_params=pltpu.CompilerParams(vmem_limit_bytes=16 * 1024 * 1024),
        cost_estimate=pl.CostEstimate(flops=flops, transcendentals=0, bytes_accessed=0),
        name=name,
    )(*args)


def core_index():
    return lax.axis_index("rows") & 1


def join_kernel(own_ref, got_ref, out_ref, wide):
    odd = (lax.axis_index("rows") >> 3) & 1
    wide[pl.ds(pl.multiple_of(odd * 8, 8), 8), :] = own_ref[...].astype(jnp.float32)
    wide[pl.ds(pl.multiple_of(8 - odd * 8, 8), 8), :] = got_ref[...].astype(jnp.float32)
    out_ref[...] = wide[...].astype(out_ref.dtype)


def join(own, got):
    shape = (16, own.shape[1])
    scratch = [pltpu.VMEM(shape, jnp.float32)]
    return call(join_kernel, "join", [(shape, VMEM)], [VMEM] * 2, (own, got), scratch)[0]


def pack_kernel(*refs):
    pieces, (mine_ref, other_ref, wide) = refs[:4], refs[4:]
    device = lax.axis_index("rows")
    ring = (device >> 1) & 3
    width = mine_ref.shape[1]
    for i, piece in enumerate(pieces):
        rows = piece[...].astype(jnp.float32)
        for j in range(2):
            place = pl.multiple_of(j * 32 + ((ring - i) & 3) * 8, 8)
            wide[pl.ds(place, 8), :] = rows[j * 8 : (j + 1) * 8, :]
    for half, out in ((device & 1, mine_ref), (1 - (device & 1), other_ref)):
        columns = pl.ds(pl.multiple_of(half * width, BLK), width)
        out[...] = wide[:, columns].astype(out.dtype)


def pack(pieces):
    width = pieces[0].shape[1]
    outs = [((64, width // 2), VMEM)] * 2
    scratch = [pltpu.VMEM((64, width), jnp.float32)]
    return call(pack_kernel, "pack", outs, [VMEM] * 4, pieces, scratch)


def slab_kernel(mine_ref, got_ref, after_ref, out_ref, wide):
    core = core_index()
    for ref, side in ((mine_ref, core), (got_ref, 1 - core)):
        rows = ref[...].astype(jnp.float32)
        for i in range(8):
            place = pl.multiple_of(i * 16 + side * 8, 8)
            wide[pl.ds(place, 8), :] = rows[i * 8 : (i + 1) * 8, :]
    out_ref[...] = wide[...].astype(out_ref.dtype)


def slab(mine, got, after):
    shape = (128, mine.shape[1])
    scratch = [pltpu.VMEM(shape, jnp.float32)]
    ins = [VMEM, VMEM, ANY]
    return call(slab_kernel, "slab", [(shape, VMEM)], ins, (mine, got, after), scratch)[0]


def split_kernel(x_ref, out_ref, sem):
    width = out_ref.shape[1]
    columns = pl.ds(pl.multiple_of((1 - core_index()) * width, BLK), width)
    copy = pltpu.make_async_copy(x_ref.at[:, columns], out_ref, sem)
    copy.start()
    copy.wait()


def split(x_states):
    shape = (x_states.shape[0], x_states.shape[1] // 2)
    scratch = [pltpu.SemaphoreType.DMA]
    return call(split_kernel, "split", [(shape, VMEM)], [HBM], (x_states,), scratch)[0]


def assemble_kernel(chunks, x_ref, partner_ref, after_ref, *rest):
    outs, sems = rest[:-1], rest[-1]
    core = core_index()
    width = sum(chunks)

    def fill(mine):
        copies, at = [], 0
        for i, n in enumerate(chunks):
            columns = pl.ds(pl.multiple_of(core * width + at, BLK), n)
            up, dn = outs[2 * i], outs[2 * i + 1]
            if mine == 0:
                targets = ((0, 512, dn, 0), (256, 256, up, 0))
            else:
                targets = ((0, 256, dn, 512), (0, 512, up, 256))
            for j, (source, rows, out, place) in enumerate(targets):
                copy = pltpu.make_async_copy(
                    x_ref.at[pl.ds(source, rows), columns],
                    out.at[pl.ds(place, rows)],
                    sems.at[2 * i + j],
                )
                copy.start()
                copies.append(copy)
            at += n
        at = 0
        for i, n in enumerate(chunks):
            up, dn = outs[2 * i], outs[2 * i + 1]
            if mine == 0:
                dn[512:768, :] = partner_ref[0:256, at : at + n]
                up[256:768, :] = partner_ref[:, at : at + n]
            else:
                dn[0:512, :] = partner_ref[:, at : at + n]
                up[0:256, :] = partner_ref[256:512, at : at + n]
            at += n
        for copy in copies:
            copy.wait()

    @pl.when(core == 0)
    def _():
        fill(0)

    @pl.when(core == 1)
    def _():
        fill(1)


def assemble(x_states, partner, after, chunks):
    outs = [((768, n), VMEM) for n in chunks for _ in range(2)]
    scratch = [pltpu.SemaphoreType.DMA((2 * len(chunks),))]
    kernel = functools.partial(assemble_kernel, chunks)
    return call(kernel, "assemble", outs, [HBM, VMEM, ANY], (x_states, partner, after), scratch)


def build_kernel(device_count, col_ref, send_ref, h_ref, after_ref, *out_refs):
    device = lax.axis_index("rows")
    for out_ref in out_refs:
        out_ref[...] = jnp.zeros_like(out_ref)
    block_count = device_count * 4
    for row in range(4):
        band, half = row // 2, row % 2
        for k in range(12):
            column = col_ref[row, k]
            owner = lax.shift_right_logical(column, 2)
            local = column & 3
            offset = ((device - owner + 2) & (device_count - 1)) - 2
            slot = jnp.clip(jnp.where(offset > 0, offset - 1, 1 - offset), 0, 3)
            counts = offset == 0
            for j in range(4):
                counts = counts | (send_ref[slot, j, owner] == local)
            shift = ((column - (device * 4 + row) + 6) & (block_count - 1)) + half
            place = pl.ds(pl.multiple_of(shift * BLK, BLK), BLK)

            @pl.when(counts)
            def _(out_ref=out_refs[band], half=half, row=row, k=k, place=place):
                out_ref[half * BLK : (half + 1) * BLK, place] = h_ref[row, k]


def build(h_blocks, col_blocks, send_list, after, device_count):
    kernel = functools.partial(build_kernel, device_count)
    args = (col_blocks, send_list.transpose(1, 2, 0), h_blocks, after)
    outs = [((PAIR, WINDOW), VMEM)] * 2
    return call(kernel, "build_bands", outs, [SMEM, SMEM, VMEM, ANY], args)


def merge_kernel(*refs):
    out_ref = refs[-1]
    core = core_index()
    for i in range(2):
        out_ref[core * 2 + i] = refs[i][...]
        out_ref[2 - core * 2 + i] = refs[2 + i][...]


def merge(own, partner):
    outs = [((4, PAIR, WINDOW), VMEM)]
    return call(merge_kernel, "merge_bands", outs, [VMEM] * 4, (*own, *partner))[0]


def times_bands(g, columns, bands, left, dn, up, right):
    edge = 768 - g * PAIR

    def dot(start, stop, states):
        return jnp.dot(bands[g, :, start:stop], states, preferred_element_type=jnp.float32)

    total = dot(edge, edge + 768, dn[:, columns])
    total += dot(edge + 768, edge + 1024, up[512:768, columns])
    if g < 3:
        total += dot(0, edge, left[g * PAIR :, columns])
    if g > 0:
        total += dot(edge + 1024, WINDOW, right[: g * PAIR, columns])
    return total


def own_rows(g, columns, dn, up):
    rows = dn[g * PAIR : (g + 1) * PAIR, columns] if g < 3 else up[512:768, columns]
    return rows.astype(jnp.float32)


def first_kernel(columns, center, half, bands, left, dn, up, right, *rest):
    out_up, out_dn = rest[-2:]
    for g in range(4):
        total = times_bands(g, columns, bands, left, dn, up, right)
        value = (total - center[0] * own_rows(g, columns, dn, up)) / half[0]
        value = value.astype(jnp.bfloat16)
        if g < 3:
            out_dn[g * PAIR : (g + 1) * PAIR, :] = value
        if g > 0:
            out_up[(g - 1) * PAIR : g * PAIR, :] = value


def second_kernel(
    columns, center, half, bands, left, dn, up, right, after, xdn, xup, out_mine, out_other, outs
):
    for g in range(4):
        total = times_bands(g, columns, bands, left, dn, up, right)
        value = 2.0 * (total - center[0] * own_rows(g, columns, dn, up)) / half[0]
        value -= own_rows(g, columns, xdn, xup)
        outs[g * PAIR : (g + 1) * PAIR, :] = value.astype(jnp.bfloat16)
    core = core_index()
    out_mine[...] = outs[pl.ds(core * 512, 512), :]
    out_other[...] = outs[pl.ds(512 - core * 512, 512), :]


def first_pass(columns, *args):
    n = columns.stop - columns.start
    outs = [((768, n), VMEM)] * 2
    ins = [SMEM] * 2 + [VMEM] * 5 + [ANY] * (len(args) - 7)
    kernel = functools.partial(first_kernel, columns)
    return call(kernel, "first_pass", outs, ins, args, flops=WORK * n // 20)


def second_pass(columns, *args):
    n = columns.stop - columns.start
    outs = [((512, n), VMEM)] * 2
    ins = [SMEM] * 2 + [VMEM] * 5 + [ANY] + [VMEM] * 2
    scratch = [pltpu.VMEM((1024, n), jnp.bfloat16)]
    kernel = functools.partial(second_kernel, columns)
    return call(kernel, "second_pass", outs, ins, args, scratch, flops=WORK * n)


def tie_kernel(*refs):
    pass


def tie(array, after):
    return call(tie_kernel, "tie", [(array.shape, ANY)], [ANY] * 2, (array, after), (), {0: 0})[0]


def stack_kernel(count, *refs):
    out, at = refs[-1], 0
    for ref in refs[:count]:
        out[at : at + ref.shape[0], :] = ref[...]
        at += ref.shape[0]


def stack(pieces, *after):
    shape = (sum(piece.shape[0] for piece in pieces), pieces[0].shape[1])
    kernel = functools.partial(stack_kernel, len(pieces))
    ins = [VMEM] * len(pieces) + [ANY] * len(after)
    return call(kernel, "stack", [(shape, VMEM)], ins, (*pieces, *after))[0]


def z_step(y):
    return 1 if y < 2 else -1


def x_step(y, z, z_count, forward):
    if forward:
        return -1 if (y == 3 and z == 0) else 1
    return 1 if (y == 0 and z == z_count - 1) else -1


def rotate_kernel(chunks, own_half, *refs):
    count = len(chunks)
    own, got, parts = refs[:count], refs[count : 2 * count], refs[2 * count : 2 * count + 2]
    out_ref, rot, outs, sems = refs[-4:]
    device = lax.axis_index("rows")
    core, y = device & 1, (device >> 1) & 3
    z, x = (device >> 3) & 7, device >> 6
    z_way = jnp.where(y < 2, 1, -1)
    ways = (
        jnp.where((y == 3) & (z == 0), -1, 1),
        jnp.where((y == 0) & (z == 7), 1, -1),
    )
    for part, pieces in zip(parts, (EARLY, LATE)):
        for at, (j, i) in enumerate(pieces):
            from_x = (x - ways[j % 2] * i) & 3
            from_z = ((z >> 1) - z_way * j) & 3
            place = pl.multiple_of(from_x * 512 + from_z * 128, 128)
            rot[pl.ds(place, 128), :] = part[at * 128 : (at + 1) * 128, :]
    width = sum(chunks)
    tile = 256
    half = core if own_half else 1 - core
    stores = []
    for t in range(width // tile):
        columns = slice(t * tile, (t + 1) * tile)
        total, at = 0.0, 0
        for i, n in enumerate(chunks):
            for piece, side in ((own[i], core), (got[i], 1 - core)):
                rows = pl.ds(pl.multiple_of(side * width + at, BLK), n)
                total += jnp.dot(piece[...], rot[rows, columns], preferred_element_type=jnp.float32)
            at += n
        outs[:, columns] = total.astype(jnp.bfloat16)
        target = pl.ds(pl.multiple_of(half * width + t * tile, BLK), tile)
        stores.append(
            pltpu.make_async_copy(outs.at[:, columns], out_ref.at[:, target], sems.at[t])
        )
        stores[-1].start()
    for store in stores:
        store.wait()


def rotate(own, got, parts, chunks, out=None):
    width = sum(chunks)
    kernel = functools.partial(rotate_kernel, chunks, out is None)
    args, ins = [*own, *got, *parts], [VMEM] * (2 * len(chunks) + 2)
    aliases = None
    if out is not None:
        aliases = {len(args): 0}
        args.append(out)
        ins.append(HBM)
    scratch = [
        pltpu.VMEM((2 * width, width), jnp.bfloat16),
        pltpu.VMEM((512, width), jnp.bfloat16),
        pltpu.SemaphoreType.DMA((width // 256,)),
    ]
    return call(kernel, "rotate", [((512, 2 * width), HBM)], ins, args, scratch, aliases)[0]


def local(x_states, h_blocks, col_blocks, send_list, center, half_width, rotation):
    count = lax.axis_size("rows")
    swap = [(i, i ^ 1) for i in range(count)]
    onward = [(i, (i + 2) % count) for i in range(count)]
    backward = [(i, (i - 2) % count) for i in range(count)]

    def move(array, route):
        return lax.ppermute(array, "rows", route)

    def ring(step):
        return [(8 * (i // 8) + (i + 2 * step) % 8, i) for i in range(count)]

    def place(i):
        return i >> 6, (i >> 3) & 7, (i >> 1) & 3

    def along_z(i):
        x, z, y = place(i)
        return x * 64 + (z + 2 * z_step(y)) % 8 * 8 + i % 8

    def along_x(i, forward):
        x, z, y = place(i)
        return (x + x_step(y, z, 8, forward)) % 4 * 64 + i % 64

    z_route = [(i, along_z(i)) for i in range(count)]
    x_routes = [[(i, along_x(i, forward)) for i in range(count)] for forward in (True, False)]

    partner = move(split(x_states), swap)
    rotation = join(rotation, move(rotation, [(i, i ^ 8) for i in range(count)]))
    mine, other = pack([rotation] + [move(rotation, ring(step)) for step in (-1, -2, -3)])
    up, dn = assemble(x_states, partner, mine, (sum(CHUNKS),))
    left, right = move(up, onward), move(dn, backward)
    rows = slab(mine, move(other, swap), up)
    bands = build(h_blocks, col_blocks, send_list, rows, count)
    bands = merge(bands, [move(band, swap) for band in bands])
    slabs = [rows, tie(move(rows, z_route), bands)]
    slabs.append(move(slabs[1], z_route))
    chains = [[stack([rows], bands)], [slabs[1]], [slabs[2]]]

    def on(j, steps):
        for _ in range(steps):
            chains[j].append(move(chains[j][-1], x_routes[j % 2]))

    on(0, 3)
    on(1, 2)

    fixed = (center, half_width, bands)

    starts = [sum(CHUNKS[:i]) for i in range(len(CHUNKS))]
    columns = [slice(start, start + n) for start, n in zip(starts, CHUNKS)]
    every = slice(0, sum(CHUNKS))
    first_up, first_dn = first_pass(every, *fixed, left, dn, up, right, slabs[2], chains[0][3], chains[1][2])
    halo = (move(first_up, onward), first_dn, first_up, move(first_dn, backward))
    after = first_up
    chains[1][2], chains[2][0] = tie(chains[1][2], after), tie(chains[2][0], after)
    chains.append([move(chains[2][0], z_route)])
    on(1, 1)
    on(2, 3)
    on(3, 3)
    own, got = [], []
    for part in columns:
        mine, other = second_pass(part, *fixed, *halo, after, dn, up)
        after = mine
        own.append(mine)
        got.append(move(other, swap))
    parts = [
        stack([chains[j][i] for j, i in EARLY]),
        stack([chains[j][i] for j, i in LATE], own[-1]),
    ]
    out = rotate(own, got, parts, CHUNKS)
    return rotate(own, got, [move(part, swap) for part in parts], CHUNKS, out)


def solution(mesh):
    placed = (
        P("rows", None),
        P("rows", None, None, None),
        P("rows", None),
        P(),
        P(),
        P(),
        P("rows", None),
    )
    return jax.shard_map(
        local, mesh=mesh, in_specs=placed, out_specs=P("rows", None), check_vma=False
    )
```
